32 devices in a mesh: rep: 2 (over x), grp: 8 (over z, y), loc: 2 (over core).
Axes of the slice: x: 2, y: 2, z: 4, core: 2. Of those that a mesh axis runs over, the one named last changes fastest.
Arguments:
- grad_out: bfloat16 [8192, 3584], P(('rep', 'grp'), 'loc'), parts along dimension 0, may hold values from -0.59765625 to 0.59765625
- hidden: bfloat16 [8192, 1024], P(('rep', 'grp')), parts along dimension 0, may hold values from -6 to 6
- weights: bfloat16 [8, 1024, 3584], P('grp', None, 'loc'), may hold values from -0.1875 to 0.1875
- counts: int32 [16, 3], P(('rep', 'grp')), parts along dimension 0, may hold values from 1 to 256, 512 in all within a row
Outputs:
- grad_hidden: bfloat16 [8192, 1024], P(('rep', 'grp'), 'loc'), parts along dimension 0
- grad_weights: bfloat16 [16, 1024, 3584], P(('rep', 'grp'), None, 'loc'), parts along dimension 0
The draws below stay inside these ranges and needn't reach their ends.
There are 2 independent parts, one for each index of `rep`. The reference program is written for one: setup_inputs(seed, part) draws one part's arguments, and reference() takes and returns one part's arrays. A program takes and returns all parts, laid end to end along the dimension named above; an argument that names none is the same for every part. Nothing has to cross between parts.
Inputs may be any that keep to these rules, and one draw needn't show every extreme that they name: Each row of counts sums to 512; the largest entry of every row is exactly 256.
All inputs are finite; a program needn't handle non-finite values.
Results may differ from the reference program's by a relative error of at most 0.001.
Values may be sent and summed in bfloat16 or wider, within the bound.
No kernel may reach another device: no remote copies, remote signals or barrier semaphores. Data moves between devices by JAX's collectives and lax.ppermute only.
A program may use at most 128 MiB of HBM per device.

```python
import math
import jax
import jax.numpy as jnp
import numpy as np
from jax import lax

DW = 3584
FF = 1024
ROWS = 512
REACH = 3
CAP = 256
TOKENS = 4096
EXPERTS = 8
N_GRP = 8


def shard_levels(rng, extent, pieces, least, largest):
    def one(position, shards_of):
        heights = jax.random.uniform(jax.random.fold_in(jax.random.fold_in(rng, 6), position), (shards_of,), jnp.float32, least / len(pieces), largest / len(pieces))
        return jnp.repeat(jnp.exp(heights), extent[position] // shards_of).reshape((-1,) + (1,) * (len(extent) - position - 1))

    gain = one(*pieces[0])
    for cut in pieces[1:]:
        gain = gain * one(*cut)
    return gain


def profile(amount, total, reach, lean):
    loads = [(1 << 20) // math.isqrt(grade ** lean) + 1 for grade in range(2, amount + 1)]
    rest, given = total - reach - (amount - 1), [1] * (amount - 1)
    while rest > 0:
        movable = [i for i in range(amount - 1) if given[i] < reach]
        whole, budget = sum([loads[i] for i in movable]), rest
        for i in movable:
            extra = min(reach - given[i], max(1, budget * loads[i] // whole), rest)
            given[i] = given[i] + extra
            rest = rest - extra
    return np.array([reach] + given)


def ragged(key, amount, total, bound, lean):
    if amount == 2:
        one = jax.random.randint(key, (), max(1, total - bound), min(bound, total - 1) + 1)
        return jnp.stack([one, total - one])
    tallies = jnp.asarray(profile(amount, total, bound, lean), jnp.int32)
    twos = (amount - 1) // 2
    source_of, sink = tallies[1:1 + 2 * twos:2], tallies[2:2 + 2 * twos:2]
    slack = jnp.minimum(source_of - 1, bound - sink)
    shifted = jax.random.randint(jax.random.fold_in(key, 1), (twos,), 0, 1 << 20) % (slack + 1)
    tallies = tallies.at[1:1 + 2 * twos:2].set(source_of - shifted).at[2:2 + 2 * twos:2].set(sink + shifted)
    return tallies[jax.random.permutation(jax.random.fold_in(key, 2), amount)]


def noise(rng, dims, spread, most, cuts=(), kind=jnp.bfloat16):
    loudness = shard_levels(rng, dims, cuts, -0.22, 0.18) if cuts else 1.0
    entries = jax.random.normal(rng, dims, jnp.float32) * spread * loudness
    return jnp.minimum(jnp.maximum(entries, -most), most).astype(kind)


def setup_inputs(seed: int = 0, part: int = 0) -> dict:
    splits = jax.random.split(jax.random.key(seed), 5)
    part_keys = jax.random.split(jax.random.fold_in(splits[4], part), 5)
    return {
        "grad_out": noise(part_keys[0], (TOKENS, DW), 0.1, 0.59765625, ((0, 8), (1, 2))),
        "hidden": noise(part_keys[1], (TOKENS, FF), 1.0, 6.0, ((0, 8),)),
        "weights": noise(splits[2], (EXPERTS, FF, DW), FF ** -0.5, 0.1875, ((0, 8), (2, 2))),
        "counts": jax.vmap(lambda own: ragged(own, REACH, ROWS, CAP, 2))(jax.random.split(part_keys[3], N_GRP)).reshape((N_GRP, REACH)).astype(jnp.int32),
    }


def segment_block(grad_out, hidden, counts, device, neighbour):
    counts_row = counts[device]
    offsets = jnp.cumsum(counts_row) - counts_row
    first = offsets[neighbour].astype(jnp.int32)
    start = jnp.minimum(first, ROWS - CAP).astype(jnp.int32)
    positions = jnp.arange(CAP, dtype=jnp.int32)
    inside = (start + positions >= first) & (start + positions < first + counts_row[neighbour])
    base = (device * ROWS + start).astype(jnp.int32)
    grad_block = lax.dynamic_slice_in_dim(grad_out, base, CAP, 0)
    hidden_block = lax.dynamic_slice_in_dim(hidden, base, CAP, 0)
    grad_block = jnp.where(inside[:, None], grad_block, jnp.zeros_like(grad_block))
    hidden_block = jnp.where(inside[:, None], hidden_block, jnp.zeros_like(hidden_block))
    return (start, grad_block, hidden_block)

def reference(grad_out, hidden, weights, counts):

    def hidden_rows(device):
        total = jnp.zeros((ROWS, FF), jnp.float32)
        for neighbour in range(REACH):
            start, grad_block, hidden_block = segment_block(grad_out, hidden, counts, device, neighbour)
            expert = ((device + neighbour) % N_GRP).astype(jnp.int32)
            matrix = weights[expert]
            product = lax.dot_general(grad_block, matrix, (((1,), (1,)), ((), ())), preferred_element_type=jnp.float32)
            current = lax.dynamic_slice_in_dim(total, start, CAP, 0)
            total = lax.dynamic_update_slice_in_dim(total, current + product, start, 0)
        return total.astype(jnp.bfloat16)

    def expert_grad(expert):
        total = jnp.zeros((FF, DW), jnp.float32)
        for neighbour in range(REACH):
            device = ((expert - neighbour + N_GRP) % N_GRP).astype(jnp.int32)
            start, grad_block, hidden_block = segment_block(grad_out, hidden, counts, device, neighbour)
            total = total + lax.dot_general(hidden_block, grad_block, (((0,), (0,)), ((), ())), preferred_element_type=jnp.float32)
        return total.astype(jnp.bfloat16)
    devices = jnp.arange(N_GRP, dtype=jnp.int32)
    grad_hidden = lax.map(hidden_rows, devices).reshape(TOKENS, FF)
    grad_weights = lax.map(expert_grad, devices)
    return (grad_hidden, grad_weights)
```

```python
import jax
import jax.numpy as jnp
from jax import lax
from jax.sharding import PartitionSpec as P

CAP = 256
RELAYED = 96


def send(value, pairs):
    return lax.ppermute(value, "grp", pairs)


def swap_cores(value):
    return lax.ppermute(value, "loc", [(0, 1), (1, 0)])


def dot(left, right, contract):
    return lax.dot_general(left, right, ((contract[:1], contract[1:]), ((), ())), preferred_element_type=jnp.float32)


def picker(first, count, rows):
    place = lax.broadcasted_iota(jnp.int32, (CAP, rows), 0)
    row = lax.broadcasted_iota(jnp.int32, (CAP, rows), 1)
    return ((row == first + place) & (place < count)).astype(jnp.bfloat16)


def local(grad_out, hidden, weights, counts):
    size = lax.axis_size("grp")
    group = lax.axis_index("grp")
    core = lax.axis_index("loc")
    rows, features = grad_out.shape
    units = hidden.shape[1]
    half = units // 2
    count = counts[0]
    matrix = weights[0]
    odd = group % 2 == 1

    by1 = [(g, (g + 1) % size) for g in range(size)]
    by2 = [(g, (g + 2) % size) for g in range(size)]
    back1 = [(b, a) for a, b in by1]
    back2 = [(b, a) for a, b in by2]
    pair_swap = [(g, g ^ 1) for g in range(size)]
    even_by2 = [(g, (g + 2) % size) for g in range(0, size, 2)]

    pick0 = picker(0, count[0], rows)
    pick1 = picker(count[0], count[1], rows)
    pick2 = picker(count[0] + count[1], count[2], rows)
    hidden_half = lax.dynamic_slice_in_dim(hidden, core * half, half, 1)
    both = jnp.concatenate([grad_out, hidden_half], axis=1)
    near = dot(pick1, both, (1, 0)).astype(jnp.bfloat16)
    far_grad = dot(pick2, grad_out, (1, 0)).astype(jnp.bfloat16)
    far_hidden = dot(pick2, hidden_half, (1, 0)).astype(jnp.bfloat16)

    swapped = send(near[:RELAYED], pair_swap)
    far_grad = send(far_grad, by2)
    direct = send(near[RELAYED:], by1)
    relayed = send(swapped, even_by2)
    far_hidden = send(far_hidden, by2)
    near = jnp.concatenate([jnp.where(odd, swapped, relayed), direct], axis=0)
    near_grad, near_hidden = near[:, :features], near[:, features:]

    own_rows = lax.dynamic_slice_in_dim(matrix, core * half, half, 0)
    other_rows = lax.dynamic_slice_in_dim(matrix, (1 - core) * half, half, 0)

    def hidden_gradient(grad):
        away = swap_cores(dot(grad, other_rows, (1, 1)))
        return (dot(grad, own_rows, (1, 1)) + away).astype(jnp.bfloat16)

    own_block = hidden_gradient(grad_out[:CAP])
    far_block = send(hidden_gradient(far_grad), back2)
    near_block = send(hidden_gradient(near_grad), back1)
    placed = dot(pick0, own_block, (0, 0)) + dot(pick2, far_block, (0, 0)) + dot(pick1, near_block, (0, 0))
    grad_hidden = placed.astype(jnp.bfloat16)

    def whole(part):
        other = swap_cores(part)
        return jnp.where(core == 0, jnp.concatenate([part, other], 1), jnp.concatenate([other, part], 1))

    own_hidden = jnp.where(lax.broadcasted_iota(jnp.int32, (CAP, 1), 0) < count[0], hidden[:CAP], 0)
    total = dot(own_hidden, grad_out[:CAP], (0, 0))
    total = total + dot(whole(far_hidden), far_grad, (0, 0))
    total = total + dot(whole(near_hidden), near_grad, (0, 0))
    return grad_hidden, total.astype(jnp.bfloat16)[None]


def solution(mesh):
    return jax.shard_map(
        local,
        mesh=mesh,
        in_specs=(
            P(("rep", "grp"), "loc"),
            P(("rep", "grp"), None),
            P("grp", None, "loc"),
            P(("rep", "grp"), None),
        ),
        out_specs=(P(("rep", "grp"), "loc"), P(("rep", "grp"), None, "loc")),
        check_vma=False,
    )
```

```python
import jax
import jax.numpy as jnp
from jax import lax
from jax.experimental import pallas as pl
from jax.experimental.pallas import tpu as pltpu
from jax.sharding import PartitionSpec as P

CAP = 256
RELAYED = 128
TILE = 256
BF16, F32 = jnp.bfloat16, jnp.float32
VMEM = pl.BlockSpec(memory_space=pltpu.VMEM)
SMEM = pl.BlockSpec(memory_space=pltpu.SMEM)
ANY = pl.BlockSpec(memory_space=pl.ANY)


def call(kernel, outs, *operands, after=(), scalars=0, grid=None, out_specs=None, cost=10**10):
    def body(*refs):
        kernel(*refs[: len(operands)], *refs[len(operands) + len(after) :])

    extra = {} if grid is None else {"grid": grid}
    return pl.pallas_call(
        body,
        out_shape=[jax.ShapeDtypeStruct(shape, dtype) for shape, dtype in outs],
        in_specs=[SMEM] * scalars + [VMEM] * (len(operands) - scalars) + [ANY] * len(after),
        out_specs=[VMEM] * len(outs) if out_specs is None else out_specs,
        cost_estimate=pl.CostEstimate(flops=cost, bytes_accessed=10**3, transcendentals=0),
        compiler_params=pltpu.CompilerParams(vmem_limit_bytes=16 << 20),
        name=kernel.__name__,
        **extra,
    )(*operands, *after)


def dot(left, right, contract=(1, 0)):
    return lax.dot_general(left, right, ((contract[:1], contract[1:]), ((), ())), preferred_element_type=F32)


def half_of(which, extent):
    return pl.ds(pl.multiple_of(which * extent, extent), extent)


def segment(counts, index):
    first = jnp.int32(0)
    for earlier in range(index):
        first = first + counts[0, earlier]
    return first, counts[0, index]


def picker(counts, index, rows):
    first, count = segment(counts, index)
    place = lax.broadcasted_iota(jnp.int32, (CAP, rows), 0)
    row = lax.broadcasted_iota(jnp.int32, (CAP, rows), 1)
    return ((row == first + place) & (place < count)).astype(BF16)


def placer(counts, index, rows):
    first, count = segment(counts, index)
    row = lax.broadcasted_iota(jnp.int32, (rows, CAP), 0)
    place = lax.broadcasted_iota(jnp.int32, (rows, CAP), 1)
    return ((row == first + place) & (place < count)).astype(BF16)


def tiles(extent):
    return [slice(at, min(at + TILE, extent)) for at in range(0, extent, TILE)]


def pick_far(counts, grad_out, far):
    pick = picker(counts, 2, grad_out.shape[0])
    for tile in tiles(grad_out.shape[1]):
        far[:, tile] = dot(pick, grad_out[:, tile]).astype(BF16)


def pick_turned(counts, grad_out, turned):
    pick = picker(counts, 1, grad_out.shape[0])[:RELAYED]
    for tile in tiles(grad_out.shape[1]):
        turned[:, tile] = dot(pick, grad_out[:, tile]).astype(BF16)


def pick_direct(counts, grad_out, direct):
    pick = picker(counts, 1, grad_out.shape[0])[RELAYED:]
    for tile in tiles(grad_out.shape[1]):
        direct[:, tile] = dot(pick, grad_out[:, tile]).astype(BF16)


def pick_hidden(counts, hidden, far, near, own, places):
    rows, units = hidden.shape
    columns = half_of(lax.axis_index("loc"), units // 2)
    for index, out in ((2, far), (1, near)):
        out[...] = dot(hidden[:, columns], picker(counts, index, rows), (0, 1)).astype(BF16)
    pick = picker(counts, 0, rows)
    for tile in tiles(units):
        own[tile, :] = dot(hidden[:, tile], pick, (0, 1)).astype(BF16)
    for index in range(3):
        places[:, index * CAP : (index + 1) * CAP] = placer(counts, index, rows)


def product_away(grad, weights, away):
    half = weights.shape[1] // 2
    away[...] = dot(grad[:CAP, :], weights[0, half_of(1 - lax.axis_index("loc"), half), :], (1, 1))


def product_here(grad, weights, here):
    half = weights.shape[1] // 2
    here[...] = dot(grad[:CAP, :], weights[0, half_of(lax.axis_index("loc"), half), :], (1, 1))


def join_near(turned, relayed, direct, weights, near, away):
    odd = lax.axis_index("grp") % 2 == 1

    @pl.when(odd)
    def _():
        near[:RELAYED, :] = turned[...]

    @pl.when(jnp.logical_not(odd))
    def _():
        near[:RELAYED, :] = relayed[...]

    near[RELAYED:, :] = direct[...]
    product_away(near, weights, away)


def add_halves(here, other, out):
    out[...] = (here[...] + other[...]).astype(BF16)


def place_rows(places, own, near, far, out):
    total = dot(places[:, :CAP], own[...])
    total = total + dot(places[:, CAP : 2 * CAP], near[...])
    total = total + dot(places[:, 2 * CAP :], far[...])
    out[...] = total.astype(BF16)


def weight_gradient_here(own_hidden, far_hidden, near_hidden, own, far, near, out):
    columns = half_of(pl.program_id(0), TILE)
    rows = half_of(lax.axis_index("loc"), far_hidden.shape[0])
    total = dot(own_hidden[rows, :], own[:CAP, columns])
    total = total + dot(far_hidden[...], far[:, columns])
    total = total + dot(near_hidden[...], near[:, columns])
    out[...] = total.astype(BF16)


def weight_gradient(own_hidden, far_hidden, near_hidden, own, far, near, here, out):
    columns = half_of(pl.program_id(0), TILE)
    core = lax.axis_index("loc")
    half = far_hidden.shape[0]
    rows = half_of(1 - core, half)
    total = dot(own_hidden[rows, :], own[:CAP, columns])
    total = total + dot(far_hidden[...], far[:, columns])
    total = total + dot(near_hidden[...], near[:, columns])
    out[0, rows, :] = total.astype(BF16)
    out[0, half_of(core, half), :] = here[:, columns]


def local(grad_out, hidden, weights, counts):
    size = lax.axis_size("grp")
    rows, features = grad_out.shape
    units = hidden.shape[1]
    half = units // 2

    by1 = [(g, (g + 1) % size) for g in range(size)]
    by2 = [(g, (g + 2) % size) for g in range(size)]
    back1 = [(b, a) for a, b in by1]
    back2 = [(b, a) for a, b in by2]
    turn = [(g, g ^ 1) for g in range(size)]
    even_by2 = by2[::2]

    def send(value, pairs):
        return lax.ppermute(value, "grp", pairs)

    def swap_cores(value):
        return lax.ppermute(value, "loc", [(0, 1), (1, 0)])

    partial = ((CAP, half), F32)
    block = ((CAP, half), BF16)
    (far,) = call(pick_far, [((CAP, features), BF16)], counts, grad_out, scalars=1)
    far_in = send(far, by2)
    (turned,) = call(pick_turned, [((RELAYED, features), BF16)], counts, grad_out, scalars=1, after=(far,))
    turned_in = send(turned, turn)

    (own_away,) = call(product_away, [partial], grad_out, weights, after=(turned,))
    own_other = swap_cores(own_away)
    (own_here,) = call(product_here, [partial], grad_out, weights, after=(own_away,))
    far_hidden, near_hidden, own_hidden, places = call(
        pick_hidden,
        [((half, CAP), BF16), ((half, CAP), BF16), ((units, CAP), BF16), ((rows, 3 * CAP), BF16)],
        counts, hidden, scalars=1, after=(own_here,),
    )
    (direct,) = call(
        pick_direct, [((CAP - RELAYED, features), BF16)], counts, grad_out, scalars=1, after=(places,)
    )
    direct_in = send(direct, by1)
    (own_block,) = call(add_halves, [block], own_here, own_other, after=(direct,))

    turned_in, own_block = lax.optimization_barrier((turned_in, own_block))
    relayed_in = send(turned_in, even_by2)

    (far_away,) = call(product_away, [partial], far_in, weights, after=(turned_in,))
    far_other = swap_cores(far_away)
    (far_here,) = call(product_here, [partial], far_in, weights, after=(far_away,))
    (far_block,) = call(add_halves, [block], far_here, far_other)
    far_back = send(far_block, back2)
    far_hidden, near_hidden, far_here = lax.optimization_barrier((far_hidden, near_hidden, far_here))
    far_hidden_in = send(far_hidden, by2)
    near_hidden_in = send(near_hidden, by1)

    near_in, near_away = call(
        join_near, [((CAP, features), BF16), partial], turned_in, relayed_in, direct_in, weights, after=(far_block,)
    )
    near_other = swap_cores(near_away)
    (near_here,) = call(product_here, [partial], near_in, weights, after=(near_away,))
    (near_block,) = call(add_halves, [block], near_here, near_other)
    near_back = send(near_block, back1)

    far_hidden_in, near_hidden_in, near_block = lax.optimization_barrier((far_hidden_in, near_hidden_in, near_block))
    strips = (features // TILE,)
    (here,) = call(
        weight_gradient_here, [((half, features), BF16)],
        own_hidden, far_hidden_in, near_hidden_in, grad_out, far_in, near_in,
        grid=strips, out_specs=[pl.BlockSpec((half, TILE), lambda tile: (0, tile))],
    )
    (grad_hidden,) = call(
        place_rows, [((rows, half), BF16)], places, own_block, near_back, far_back, after=(here,)
    )
    (grad_weights,) = call(
        weight_gradient, [((1, units, features), BF16)],
        own_hidden, swap_cores(far_hidden_in), swap_cores(near_hidden_in), grad_out, far_in, near_in, here,
        grid=strips, out_specs=[pl.BlockSpec((1, units, TILE), lambda tile: (0, 0, tile))],
    )
    return grad_hidden, grad_weights


def solution(mesh):
    return jax.shard_map(
        local,
        mesh=mesh,
        in_specs=(
            P(("rep", "grp"), "loc"),
            P(("rep", "grp"), None),
            P("grp", None, "loc"),
            P(("rep", "grp"), None),
        ),
        out_specs=(P(("rep", "grp"), "loc"), P(("rep", "grp"), None, "loc")),
        check_vma=False,
    )
```

```python
import functools

import jax
import jax.numpy as jnp
from jax import lax
from jax.experimental import pallas as pl
from jax.experimental.pallas import tpu as pltpu
from jax.sharding import PartitionSpec as P

CAP = 256
RELAYED = 144
TILE = 256
BLOCK = 256
BF16, F32 = jnp.bfloat16, jnp.float32
VMEM = pl.BlockSpec(memory_space=pltpu.VMEM)
SMEM = pl.BlockSpec(memory_space=pltpu.SMEM)
ANY = pl.BlockSpec(memory_space=pl.ANY)


def call(kernel, outs, *operands, after=(), scalars=0, grid=None, out_specs=None, cost=10**10):
    def body(*refs):
        kernel(*refs[: len(operands)], *refs[len(operands) + len(after) :])

    extra = {} if grid is None else {"grid": grid}
    return pl.pallas_call(
        body,
        out_shape=[jax.ShapeDtypeStruct(shape, dtype) for shape, dtype in outs],
        in_specs=[SMEM] * scalars + [VMEM] * (len(operands) - scalars) + [ANY] * len(after),
        out_specs=[VMEM] * len(outs) if out_specs is None else out_specs,
        cost_estimate=pl.CostEstimate(flops=cost, bytes_accessed=10**3, transcendentals=0),
        compiler_params=pltpu.CompilerParams(vmem_limit_bytes=16 << 20),
        name=kernel.__name__,
        **extra,
    )(*operands, *after)


def dot(left, right, contract=(1, 0)):
    return lax.dot_general(left, right, ((contract[:1], contract[1:]), ((), ())), preferred_element_type=F32)


def half_of(which, extent):
    return pl.ds(pl.multiple_of(which * extent, extent), extent)


def segment(counts, index):
    first = jnp.int32(0)
    for earlier in range(index):
        first = first + counts[0, earlier]
    return first, counts[0, index]


def picker(counts, index, rows):
    first, count = segment(counts, index)
    place = lax.broadcasted_iota(jnp.int32, (CAP, rows), 0)
    row = lax.broadcasted_iota(jnp.int32, (CAP, rows), 1)
    return ((row == first + place) & (place < count)).astype(BF16)


def placer(counts, index, rows):
    first, count = segment(counts, index)
    row = lax.broadcasted_iota(jnp.int32, (rows, CAP), 0)
    place = lax.broadcasted_iota(jnp.int32, (rows, CAP), 1)
    return ((row == first + place) & (place < count)).astype(BF16)


def tiles(extent):
    return [slice(at, min(at + TILE, extent)) for at in range(0, extent, TILE)]


def pick_far(counts, grad_out, far):
    pick = picker(counts, 2, grad_out.shape[0])
    for tile in tiles(grad_out.shape[1]):
        far[:, tile] = dot(pick, grad_out[:, tile]).astype(BF16)


def pick_turned(counts, grad_out, turned):
    pick = picker(counts, 1, grad_out.shape[0])[:RELAYED]
    for tile in tiles(grad_out.shape[1]):
        turned[:, tile] = dot(pick, grad_out[:, tile]).astype(BF16)


def pick_direct(counts, grad_out, direct):
    pick = picker(counts, 1, grad_out.shape[0])[RELAYED:]
    for tile in tiles(grad_out.shape[1]):
        direct[:, tile] = dot(pick, grad_out[:, tile]).astype(BF16)


def pick_hidden(counts, hidden, far, near, own, places):
    rows, units = hidden.shape
    columns = half_of(lax.axis_index("loc"), units // 2)
    for index, out in ((2, far), (1, near)):
        out[...] = dot(hidden[:, columns], picker(counts, index, rows), (0, 1)).astype(BF16)
    pick = picker(counts, 0, rows)
    for tile in tiles(units):
        own[tile, :] = dot(hidden[:, tile], pick, (0, 1)).astype(BF16)
    for index in range(3):
        places[:, index * CAP : (index + 1) * CAP] = placer(counts, index, rows)


def product_away(grad, weights, away):
    half = weights.shape[1] // 2
    away[...] = dot(grad[:CAP, :], weights[0, half_of(1 - lax.axis_index("loc"), half), :], (1, 1))


def product_here(grad, weights, here):
    half = weights.shape[1] // 2
    here[...] = dot(grad[:CAP, :], weights[0, half_of(lax.axis_index("loc"), half), :], (1, 1))


def join_near(turned, relayed, direct, weights, near, away):
    odd = lax.axis_index("grp") % 2 == 1

    @pl.when(odd)
    def _():
        near[:RELAYED, :] = turned[...]

    @pl.when(jnp.logical_not(odd))
    def _():
        near[:RELAYED, :] = relayed[...]

    near[RELAYED:, :] = direct[...]
    product_away(near, weights, away)


def add_halves(here, other, out):
    out[...] = (here[...] + other[...]).astype(BF16)


def place_rows(places, own, near, far, out):
    total = dot(places[:, :CAP], own[...])
    total = total + dot(places[:, CAP : 2 * CAP], near[...])
    total = total + dot(places[:, 2 * CAP :], far[...])
    out[...] = total.astype(BF16)


def half_weights(side, own_hidden, far_hidden, near_hidden, own, far, near, *refs):
    out, token = refs[-2:]
    step = pl.program_id(0)
    rows = half_of(step, BLOCK)
    whole = half_of(side() * (far_hidden.shape[0] // BLOCK) + step, BLOCK)
    for tile in tiles(far.shape[1]):
        total = dot(own_hidden[whole, :], own[:CAP, tile])
        total = total + dot(far_hidden[rows, :], far[:, tile])
        out[0, :, tile] = (total + dot(near_hidden[rows, :], near[:, tile])).astype(BF16)
    token[...] = jnp.zeros_like(token)


def rows_of_half(side, *operands, units, features, before=()):
    steps = units // 2 // BLOCK
    return pl.pallas_call(
        functools.partial(half_weights, side),
        out_shape=[jax.ShapeDtypeStruct((1, units, features), BF16), jax.ShapeDtypeStruct((16, 128), BF16)],
        grid=(steps,),
        in_specs=[VMEM] * len(operands) + [ANY] * len(before),
        out_specs=[pl.BlockSpec((1, BLOCK, features), lambda step: (0, side() * steps + step, 0)), VMEM],
        input_output_aliases={len(operands): 0} if before else {},
        cost_estimate=pl.CostEstimate(flops=10**10, bytes_accessed=10**3, transcendentals=0),
        compiler_params=pltpu.CompilerParams(vmem_limit_bytes=16 << 20),
        name="half_weights",
    )(*operands, *before)


def local(grad_out, hidden, weights, counts):
    size = lax.axis_size("grp")
    rows, features = grad_out.shape
    units = hidden.shape[1]
    half = units // 2

    by1 = [(g, (g + 1) % size) for g in range(size)]
    by2 = [(g, (g + 2) % size) for g in range(size)]
    back1 = [(b, a) for a, b in by1]
    back2 = [(b, a) for a, b in by2]
    turn = [(g, g ^ 1) for g in range(size)]
    even_by2 = by2[::2]

    def send(value, pairs):
        return lax.ppermute(value, "grp", pairs)

    def swap_cores(value):
        return lax.ppermute(value, "loc", [(0, 1), (1, 0)])

    partial = ((CAP, half), F32)
    block = ((CAP, half), BF16)
    (far,) = call(pick_far, [((CAP, features), BF16)], counts, grad_out, scalars=1)
    far_in = send(far, by2)
    (turned,) = call(pick_turned, [((RELAYED, features), BF16)], counts, grad_out, scalars=1, after=(far,))
    turned_in = send(turned, turn)

    (own_away,) = call(product_away, [partial], grad_out, weights, after=(turned,))
    own_other = swap_cores(own_away)
    (own_here,) = call(product_here, [partial], grad_out, weights, after=(own_away,))
    far_hidden, near_hidden, own_hidden, places = call(
        pick_hidden,
        [((half, CAP), BF16), ((half, CAP), BF16), ((units, CAP), BF16), ((rows, 3 * CAP), BF16)],
        counts, hidden, scalars=1, after=(own_here,),
    )
    (direct,) = call(
        pick_direct, [((CAP - RELAYED, features), BF16)], counts, grad_out, scalars=1, after=(places,)
    )
    direct_in = send(direct, by1)
    (own_block,) = call(add_halves, [block], own_here, own_other, after=(direct,))

    turned_in, own_block = lax.optimization_barrier((turned_in, own_block))
    relayed_in = send(turned_in, even_by2)

    (far_away,) = call(product_away, [partial], far_in, weights, after=(turned_in,))
    far_other = swap_cores(far_away)
    (far_here,) = call(product_here, [partial], far_in, weights, after=(far_away,))
    far_hidden, near_hidden, far_here = lax.optimization_barrier((far_hidden, near_hidden, far_here))
    far_hidden_in = send(far_hidden, by2)
    near_hidden_in = send(near_hidden, by1)

    near_in, near_away = call(
        join_near, [((CAP, features), BF16), partial], turned_in, relayed_in, direct_in, weights, after=(far_here,)
    )
    near_other = swap_cores(near_away)
    (near_here,) = call(product_here, [partial], near_in, weights, after=(near_away,))
    (near_block,) = call(add_halves, [block], near_here, near_other)
    near_back = send(near_block, back1)
    (far_block,) = call(add_halves, [block], far_here, far_other, after=(near_block,))
    far_back = send(far_block, back2)

    far_hidden_in, near_hidden_in, far_block = lax.optimization_barrier((far_hidden_in, near_hidden_in, far_block))
    here, _ = rows_of_half(
        lambda: lax.axis_index("loc"), own_hidden, far_hidden_in, near_hidden_in, grad_out, far_in, near_in, units=units, features=features
    )
    grad_weights, done = rows_of_half(
        lambda: 1 - lax.axis_index("loc"), own_hidden, swap_cores(far_hidden_in), swap_cores(near_hidden_in), grad_out, far_in, near_in,
        units=units, features=features, before=(here,),
    )
    (grad_hidden,) = call(
        place_rows, [((rows, half), BF16)], places, own_block, near_back, far_back, after=(done,)
    )
    return grad_hidden, grad_weights


def solution(mesh):
    return jax.shard_map(
        local,
        mesh=mesh,
        in_specs=(
            P(("rep", "grp"), "loc"),
            P(("rep", "grp"), None),
            P("grp", None, "loc"),
            P(("rep", "grp"), None),
        ),
        out_specs=(P(("rep", "grp"), "loc"), P(("rep", "grp"), None, "loc")),
        check_vma=False,
    )
```

```python
import functools

import jax
import jax.numpy as jnp
from jax import lax
from jax.experimental import pallas as pl
from jax.experimental.pallas import tpu as pltpu
from jax.sharding import PartitionSpec as P

CAP = 256
RELAYED = 144
LAST = 2
TILE = 256
BLOCK = 256
BF16, F32 = jnp.bfloat16, jnp.float32
VMEM = pl.BlockSpec(memory_space=pltpu.VMEM)
SMEM = pl.BlockSpec(memory_space=pltpu.SMEM)
ANY = pl.BlockSpec(memory_space=pl.ANY)


def call(kernel, outs, *operands, after=(), scalars=0, grid=None, out_specs=None, cost=10**10):
    def body(*refs):
        kernel(*refs[: len(operands)], *refs[len(operands) + len(after) :])

    extra = {} if grid is None else {"grid": grid}
    return pl.pallas_call(
        body,
        out_shape=[jax.ShapeDtypeStruct(shape, dtype) for shape, dtype in outs],
        in_specs=[SMEM] * scalars + [VMEM] * (len(operands) - scalars) + [ANY] * len(after),
        out_specs=[VMEM] * len(outs) if out_specs is None else out_specs,
        cost_estimate=pl.CostEstimate(flops=cost, bytes_accessed=10**3, transcendentals=0),
        compiler_params=pltpu.CompilerParams(vmem_limit_bytes=16 << 20),
        name=kernel.__name__,
        **extra,
    )(*operands, *after)


def dot(left, right, contract=(1, 0)):
    return lax.dot_general(left, right, ((contract[:1], contract[1:]), ((), ())), preferred_element_type=F32)


def half_of(which, extent):
    return pl.ds(pl.multiple_of(which * extent, extent), extent)


def segment(counts, index):
    first = jnp.int32(0)
    for earlier in range(index):
        first = first + counts[0, earlier]
    return first, counts[0, index]


def picked(counts, index, place, row, rows):
    first, count = segment(counts, index)
    if index == LAST:
        return (row == rows - CAP + place) & (place >= CAP - count)
    return (row == first + place) & (place < count)


def picker(counts, index, rows):
    place = lax.broadcasted_iota(jnp.int32, (CAP, rows), 0)
    row = lax.broadcasted_iota(jnp.int32, (CAP, rows), 1)
    return picked(counts, index, place, row, rows).astype(BF16)


def placer(counts, index, rows):
    row = lax.broadcasted_iota(jnp.int32, (rows, CAP), 0)
    place = lax.broadcasted_iota(jnp.int32, (rows, CAP), 1)
    return picked(counts, index, place, row, rows).astype(BF16)


def tiles(extent):
    return [slice(at, min(at + TILE, extent)) for at in range(0, extent, TILE)]


def pick_turned(counts, grad_out, turned):
    pick = picker(counts, 1, grad_out.shape[0])[:RELAYED]
    for tile in tiles(grad_out.shape[1]):
        turned[:, tile] = dot(pick, grad_out[:, tile]).astype(BF16)


def pick_direct(counts, grad_out, direct):
    pick = picker(counts, 1, grad_out.shape[0])[RELAYED:]
    for tile in tiles(grad_out.shape[1]):
        direct[:, tile] = dot(pick, grad_out[:, tile]).astype(BF16)


def pick_hidden(counts, hidden, far, near, own, places):
    rows, units = hidden.shape
    columns = half_of(lax.axis_index("loc"), units // 2)
    for index, out in ((2, far), (1, near)):
        out[...] = dot(hidden[:, columns], picker(counts, index, rows), (0, 1)).astype(BF16)
    pick = picker(counts, 0, rows)
    for tile in tiles(units):
        own[tile, :] = dot(hidden[:, tile], pick, (0, 1)).astype(BF16)
    for index in range(3):
        places[:, index * CAP : (index + 1) * CAP] = placer(counts, index, rows)


def product_away(grad, weights, away):
    half = weights.shape[1] // 2
    away[...] = dot(grad[:CAP, :], weights[0, half_of(1 - lax.axis_index("loc"), half), :], (1, 1))


def product_here(grad, weights, here):
    half = weights.shape[1] // 2
    here[...] = dot(grad[:CAP, :], weights[0, half_of(lax.axis_index("loc"), half), :], (1, 1))


def join_near(turned, relayed, direct, weights, near, away):
    odd = lax.axis_index("grp") % 2 == 1

    @pl.when(odd)
    def _():
        near[:RELAYED, :] = turned[...]

    @pl.when(jnp.logical_not(odd))
    def _():
        near[:RELAYED, :] = relayed[...]

    near[RELAYED:, :] = direct[...]
    product_away(near, weights, away)


def add_halves(here, other, out):
    out[...] = (here[...] + other[...]).astype(BF16)


def place_rows(places, own, near, far, out):
    total = dot(places[:, :CAP], own[...])
    total = total + dot(places[:, CAP : 2 * CAP], near[...])
    total = total + dot(places[:, 2 * CAP :], far[...])
    out[...] = total.astype(BF16)


def half_weights(side, own_hidden, far_hidden, near_hidden, own, far, near, *refs):
    out, token = refs[-2:]
    step = pl.program_id(0)
    rows = half_of(step, BLOCK)
    whole = half_of(side() * (far_hidden.shape[0] // BLOCK) + step, BLOCK)
    for tile in tiles(far.shape[1]):
        total = dot(own_hidden[whole, :], own[:CAP, tile])
        total = total + dot(far_hidden[rows, :], far[:, tile])
        out[0, :, tile] = (total + dot(near_hidden[rows, :], near[:, tile])).astype(BF16)
    token[...] = jnp.zeros_like(token)


def rows_of_half(side, *operands, units, features, before=()):
    steps = units // 2 // BLOCK
    return pl.pallas_call(
        functools.partial(half_weights, side),
        out_shape=[jax.ShapeDtypeStruct((1, units, features), BF16), jax.ShapeDtypeStruct((16, 128), BF16)],
        grid=(steps,),
        in_specs=[VMEM] * len(operands) + [ANY] * len(before),
        out_specs=[pl.BlockSpec((1, BLOCK, features), lambda step: (0, side() * steps + step, 0)), VMEM],
        input_output_aliases={len(operands): 0} if before else {},
        cost_estimate=pl.CostEstimate(flops=10**10, bytes_accessed=10**3, transcendentals=0),
        compiler_params=pltpu.CompilerParams(vmem_limit_bytes=16 << 20),
        name="half_weights",
    )(*operands, *before)


def local(grad_out, hidden, weights, counts):
    size = lax.axis_size("grp")
    rows, features = grad_out.shape
    units = hidden.shape[1]
    half = units // 2

    by1 = [(g, (g + 1) % size) for g in range(size)]
    by2 = [(g, (g + 2) % size) for g in range(size)]
    back1 = [(b, a) for a, b in by1]
    back2 = [(b, a) for a, b in by2]
    turn = [(g, g ^ 1) for g in range(size)]
    even_by2 = by2[::2]

    def send(value, pairs):
        return lax.ppermute(value, "grp", pairs)

    def swap_cores(value):
        return lax.ppermute(value, "loc", [(0, 1), (1, 0)])

    partial = ((CAP, half), F32)
    block = ((CAP, half), BF16)
    far = grad_out[rows - CAP :]
    far_in = send(far, by2)
    (turned,) = call(pick_turned, [((RELAYED, features), BF16)], counts, grad_out, scalars=1, after=(far,))
    turned_in = send(turned, turn)

    (own_away,) = call(product_away, [partial], grad_out, weights, after=(turned,))
    own_other = swap_cores(own_away)
    (own_here,) = call(product_here, [partial], grad_out, weights, after=(own_away,))
    far_hidden, near_hidden, own_hidden, places = call(
        pick_hidden,
        [((half, CAP), BF16), ((half, CAP), BF16), ((units, CAP), BF16), ((rows, 3 * CAP), BF16)],
        counts, hidden, scalars=1, after=(own_here,),
    )
    (direct,) = call(
        pick_direct, [((CAP - RELAYED, features), BF16)], counts, grad_out, scalars=1, after=(places,)
    )
    direct_in = send(direct, by1)
    (own_block,) = call(add_halves, [block], own_here, own_other, after=(direct,))

    turned_in, own_block = lax.optimization_barrier((turned_in, own_block))
    relayed_in = send(turned_in, even_by2)

    (far_away,) = call(product_away, [partial], far_in, weights, after=(turned_in,))
    far_other = swap_cores(far_away)
    (far_here,) = call(product_here, [partial], far_in, weights, after=(far_away,))
    far_hidden, near_hidden, far_here = lax.optimization_barrier((far_hidden, near_hidden, far_here))
    near_hidden_in = send(near_hidden, by1)
    far_hidden_in = send(far_hidden, by2)

    near_in, near_away = call(
        join_near, [((CAP, features), BF16), partial], turned_in, relayed_in, direct_in, weights, after=(far_here,)
    )
    near_other = swap_cores(near_away)
    (near_here,) = call(product_here, [partial], near_in, weights, after=(near_away,))
    (near_block,) = call(add_halves, [block], near_here, near_other)
    near_back = send(near_block, back1)
    (far_block,) = call(add_halves, [block], far_here, far_other, after=(near_block,))
    far_back = send(far_block, back2)

    near_hidden_in, far_hidden_in, far_block = lax.optimization_barrier((near_hidden_in, far_hidden_in, far_block))
    here, _ = rows_of_half(
        lambda: lax.axis_index("loc"), own_hidden, far_hidden_in, near_hidden_in, grad_out, far_in, near_in, units=units, features=features
    )
    grad_weights, done = rows_of_half(
        lambda: 1 - lax.axis_index("loc"), own_hidden, swap_cores(far_hidden_in), swap_cores(near_hidden_in), grad_out, far_in, near_in,
        units=units, features=features, before=(here,),
    )
    (grad_hidden,) = call(
        place_rows, [((rows, half), BF16)], places, own_block, near_back, far_back, after=(done,)
    )
    return grad_hidden, grad_weights


def solution(mesh):
    return jax.shard_map(
        local,
        mesh=mesh,
        in_specs=(
            P(("rep", "grp"), "loc"),
            P(("rep", "grp"), None),
            P("grp", None, "loc"),
            P(("rep", "grp"), None),
        ),
        out_specs=(P(("rep", "grp"), "loc"), P(("rep", "grp"), None, "loc")),
        check_vma=False,
    )
```

```python
import functools

import jax
import jax.numpy as jnp
from jax import lax
from jax.experimental import pallas as pl
from jax.experimental.pallas import tpu as pltpu
from jax.sharding import PartitionSpec as P

CAP = 256
RELAYED = 128
LAST = 2
TILE = 256
BLOCK = 256
BF16, F32 = jnp.bfloat16, jnp.float32
VMEM = pl.BlockSpec(memory_space=pltpu.VMEM)
SMEM = pl.BlockSpec(memory_space=pltpu.SMEM)
ANY = pl.BlockSpec(memory_space=pl.ANY)


def call(kernel, outs, *operands, after=(), scalars=0, grid=None, out_specs=None, cost=10**10):
    def body(*refs):
        kernel(*refs[: len(operands)], *refs[len(operands) + len(after) :])

    extra = {} if grid is None else {"grid": grid}
    return pl.pallas_call(
        body,
        out_shape=[jax.ShapeDtypeStruct(shape, dtype) for shape, dtype in outs],
        in_specs=[SMEM] * scalars + [VMEM] * (len(operands) - scalars) + [ANY] * len(after),
        out_specs=[VMEM] * len(outs) if out_specs is None else out_specs,
        cost_estimate=pl.CostEstimate(flops=cost, bytes_accessed=10**3, transcendentals=0),
        compiler_params=pltpu.CompilerParams(vmem_limit_bytes=16 << 20),
        name=kernel.__name__,
        **extra,
    )(*operands, *after)


def dot(left, right, contract=(1, 0)):
    return lax.dot_general(left, right, ((contract[:1], contract[1:]), ((), ())), preferred_element_type=F32)


def half_of(which, extent):
    return pl.ds(pl.multiple_of(which * extent, extent), extent)


def segment(counts, index):
    first = jnp.int32(0)
    for earlier in range(index):
        first = first + counts[0, earlier]
    return first, counts[0, index]


def picked(counts, index, place, row, rows):
    first, count = segment(counts, index)
    if index == LAST:
        return (row == rows - CAP + place) & (place >= CAP - count)
    return (row == first + place) & (place < count)


def picker(counts, index, rows):
    place = lax.broadcasted_iota(jnp.int32, (CAP, rows), 0)
    row = lax.broadcasted_iota(jnp.int32, (CAP, rows), 1)
    return picked(counts, index, place, row, rows).astype(BF16)


def placer(counts, index, rows):
    row = lax.broadcasted_iota(jnp.int32, (rows, CAP), 0)
    place = lax.broadcasted_iota(jnp.int32, (rows, CAP), 1)
    return picked(counts, index, place, row, rows).astype(BF16)


def tiles(extent):
    return [slice(at, min(at + TILE, extent)) for at in range(0, extent, TILE)]


def pick_turned(counts, grad_out, turned):
    pick = picker(counts, 1, grad_out.shape[0])[:RELAYED]
    for tile in tiles(grad_out.shape[1]):
        turned[:, tile] = dot(pick, grad_out[:, tile]).astype(BF16)


def pick_direct(counts, grad_out, direct):
    pick = picker(counts, 1, grad_out.shape[0])[RELAYED:]
    for tile in tiles(grad_out.shape[1]):
        direct[:, tile] = dot(pick, grad_out[:, tile]).astype(BF16)


def pick_hidden(counts, hidden, far, near):
    rows, units = hidden.shape
    columns = half_of(lax.axis_index("loc"), units // 2)
    for index, out in ((2, far), (1, near)):
        out[...] = dot(hidden[:, columns], picker(counts, index, rows), (0, 1)).astype(BF16)


def pick_own(counts, hidden, own, places):
    rows, units = hidden.shape
    pick = picker(counts, 0, rows)
    for tile in tiles(units):
        own[tile, :] = dot(hidden[:, tile], pick, (0, 1)).astype(BF16)
    for index in range(3):
        places[:, index * CAP : (index + 1) * CAP] = placer(counts, index, rows)


def product_away(grad, weights, away):
    half = weights.shape[1] // 2
    away[...] = dot(grad[:CAP, :], weights[0, half_of(1 - lax.axis_index("loc"), half), :], (1, 1))


def product_here(grad, weights, here):
    half = weights.shape[1] // 2
    here[...] = dot(grad[:CAP, :], weights[0, half_of(lax.axis_index("loc"), half), :], (1, 1))


def join_near(turned, relayed, direct, weights, near, away):
    odd = lax.axis_index("grp") % 2 == 1

    @pl.when(odd)
    def _():
        near[:RELAYED, :] = turned[...]

    @pl.when(jnp.logical_not(odd))
    def _():
        near[:RELAYED, :] = relayed[...]

    near[RELAYED:, :] = direct[...]
    product_away(near, weights, away)


def add_halves(here, other, out):
    out[...] = (here[...] + other[...]).astype(BF16)


def place_first(places, own, near, out):
    total = dot(places[:, :CAP], own[...])
    out[...] = (total + dot(places[:, CAP : 2 * CAP], near[...])).astype(BF16)


def place_last(places, first, far, out):
    out[...] = (first[...].astype(F32) + dot(places[:, 2 * CAP :], far[...])).astype(BF16)


def own_weights(own_hidden, own, total):
    for tile in tiles(own.shape[1]):
        total[:, tile] = dot(own_hidden[...], own[:CAP, tile])


def half_weights(side, far_hidden, near_hidden, far, near, before, *refs):
    out, token = refs[-2:]
    step = pl.program_id(0)
    rows = half_of(step, BLOCK)
    whole = half_of(side() * (far_hidden.shape[0] // BLOCK) + step, BLOCK)
    for tile in tiles(far.shape[1]):
        total = before[whole, tile] + dot(far_hidden[rows, :], far[:, tile])
        out[0, :, tile] = (total + dot(near_hidden[rows, :], near[:, tile])).astype(BF16)
    token[...] = jnp.zeros_like(token)


def rows_of_half(side, *operands, units, features, before=()):
    steps = units // 2 // BLOCK
    return pl.pallas_call(
        functools.partial(half_weights, side),
        out_shape=[jax.ShapeDtypeStruct((1, units, features), BF16), jax.ShapeDtypeStruct((16, 128), BF16)],
        grid=(steps,),
        in_specs=[VMEM] * len(operands) + [ANY] * len(before),
        out_specs=[pl.BlockSpec((1, BLOCK, features), lambda step: (0, side() * steps + step, 0)), VMEM],
        input_output_aliases={len(operands): 0} if before else {},
        cost_estimate=pl.CostEstimate(flops=10**10, bytes_accessed=10**3, transcendentals=0),
        compiler_params=pltpu.CompilerParams(vmem_limit_bytes=16 << 20),
        name="half_weights",
    )(*operands, *before)


def local(grad_out, hidden, weights, counts):
    size = lax.axis_size("grp")
    rows, features = grad_out.shape
    units = hidden.shape[1]
    half = units // 2

    by1 = [(g, (g + 1) % size) for g in range(size)]
    by2 = [(g, (g + 2) % size) for g in range(size)]
    back1 = [(b, a) for a, b in by1]
    back2 = [(b, a) for a, b in by2]
    turn = [(g, g ^ 1) for g in range(size)]
    even_by2 = by2[::2]

    def send(value, pairs):
        return lax.ppermute(value, "grp", pairs)

    def swap_cores(value):
        return lax.ppermute(value, "loc", [(0, 1), (1, 0)])

    partial = ((CAP, half), F32)
    block = ((CAP, half), BF16)
    far = grad_out[rows - CAP :]
    far_in = send(far, by2)
    (turned,) = call(pick_turned, [((RELAYED, features), BF16)], counts, grad_out, scalars=1, after=(far,))
    turned_in = send(turned, turn)

    (own_away,) = call(product_away, [partial], grad_out, weights, after=(turned,))
    own_other = swap_cores(own_away)
    (own_here,) = call(product_here, [partial], grad_out, weights, after=(own_away,))
    far_hidden, near_hidden = call(
        pick_hidden, [((half, CAP), BF16), ((half, CAP), BF16)], counts, hidden, scalars=1, after=(own_here,)
    )
    (direct,) = call(
        pick_direct, [((CAP - RELAYED, features), BF16)], counts, grad_out, scalars=1, after=(far_hidden,)
    )
    direct_in = send(direct, by1)
    (own_block,) = call(add_halves, [block], own_here, own_other, after=(direct,))

    turned_in, own_block = lax.optimization_barrier((turned_in, own_block))
    relayed_in = send(turned_in, even_by2)

    (far_away,) = call(product_away, [partial], far_in, weights, after=(turned_in,))
    far_other = swap_cores(far_away)
    (far_here,) = call(product_here, [partial], far_in, weights, after=(far_away,))
    far_hidden, near_hidden, far_here = lax.optimization_barrier((far_hidden, near_hidden, far_here))
    near_hidden_in = send(near_hidden, by1)
    far_hidden_in = send(far_hidden, by2)

    near_in, near_away = call(
        join_near, [((CAP, features), BF16), partial], turned_in, relayed_in, direct_in, weights, after=(far_here,)
    )
    near_other = swap_cores(near_away)
    (near_here,) = call(product_here, [partial], near_in, weights, after=(near_away,))
    (near_block,) = call(add_halves, [block], near_here, near_other)
    near_back = send(near_block, back1)
    own_hidden, places = call(
        pick_own, [((units, CAP), BF16), ((rows, 3 * CAP), BF16)], counts, hidden, scalars=1, after=(near_block,)
    )
    (total,) = call(own_weights, [((units, features), F32)], own_hidden, grad_out)
    (far_block,) = call(add_halves, [block], far_here, far_other, after=(total,))
    far_back = send(far_block, back2)

    near_hidden_in, far_hidden_in, far_block = lax.optimization_barrier((near_hidden_in, far_hidden_in, far_block))
    here, _ = rows_of_half(
        lambda: lax.axis_index("loc"), far_hidden_in, near_hidden_in, far_in, near_in, total, units=units, features=features
    )
    grad_weights, done = rows_of_half(
        lambda: 1 - lax.axis_index("loc"), swap_cores(far_hidden_in), swap_cores(near_hidden_in), far_in, near_in, total,
        units=units, features=features, before=(here,),
    )
    (placed,) = call(place_first, [((rows, half), BF16)], places, own_block, near_back, after=(done,))
    (grad_hidden,) = call(place_last, [((rows, half), BF16)], places, placed, far_back)
    return grad_hidden, grad_weights


def solution(mesh):
    return jax.shard_map(
        local,
        mesh=mesh,
        in_specs=(
            P(("rep", "grp"), "loc"),
            P(("rep", "grp"), None),
            P("grp", None, "loc"),
            P(("rep", "grp"), None),
        ),
        out_specs=(P(("rep", "grp"), "loc"), P(("rep", "grp"), None, "loc")),
        check_vma=False,
    )
```

```python
import functools

import jax
import jax.numpy as jnp
from jax import lax
from jax.experimental import pallas as pl
from jax.experimental.pallas import tpu as pltpu
from jax.sharding import PartitionSpec as P

CAP = 256
RELAYED = 128
LAST = 2
TILE = 256
BLOCK = 256
BF16, F32 = jnp.bfloat16, jnp.float32
VMEM = pl.BlockSpec(memory_space=pltpu.VMEM)
SMEM = pl.BlockSpec(memory_space=pltpu.SMEM)
ANY = pl.BlockSpec(memory_space=pl.ANY)


def call(kernel, outs, *operands, after=(), scalars=0, grid=None, out_specs=None, cost=10**10):
    def body(*refs):
        kernel(*refs[: len(operands)], *refs[len(operands) + len(after) :])

    extra = {} if grid is None else {"grid": grid}
    return pl.pallas_call(
        body,
        out_shape=[jax.ShapeDtypeStruct(shape, dtype) for shape, dtype in outs],
        in_specs=[SMEM] * scalars + [VMEM] * (len(operands) - scalars) + [ANY] * len(after),
        out_specs=[VMEM] * len(outs) if out_specs is None else out_specs,
        cost_estimate=pl.CostEstimate(flops=cost, bytes_accessed=10**3, transcendentals=0),
        compiler_params=pltpu.CompilerParams(vmem_limit_bytes=16 << 20),
        name=kernel.__name__,
        **extra,
    )(*operands, *after)


def dot(left, right, contract=(1, 0)):
    return lax.dot_general(left, right, ((contract[:1], contract[1:]), ((), ())), preferred_element_type=F32)


def half_of(which, extent):
    return pl.ds(pl.multiple_of(which * extent, extent), extent)


def segment(counts, index):
    first = jnp.int32(0)
    for earlier in range(index):
        first = first + counts[0, earlier]
    return first, counts[0, index]


def picked(counts, index, place, row, rows):
    first, count = segment(counts, index)
    if index == LAST:
        return (row == rows - CAP + place) & (place >= CAP - count)
    return (row == first + place) & (place < count)


def picker(counts, index, rows):
    place = lax.broadcasted_iota(jnp.int32, (CAP, rows), 0)
    row = lax.broadcasted_iota(jnp.int32, (CAP, rows), 1)
    return picked(counts, index, place, row, rows).astype(BF16)


def placer(counts, index, rows):
    row = lax.broadcasted_iota(jnp.int32, (rows, CAP), 0)
    place = lax.broadcasted_iota(jnp.int32, (rows, CAP), 1)
    return picked(counts, index, place, row, rows).astype(BF16)


def tiles(extent):
    return [slice(at, min(at + TILE, extent)) for at in range(0, extent, TILE)]


def pick_turned(counts, grad_out, turned):
    pick = picker(counts, 1, grad_out.shape[0])[:RELAYED]
    for tile in tiles(grad_out.shape[1]):
        turned[:, tile] = dot(pick, grad_out[:, tile]).astype(BF16)


def pick_direct(counts, grad_out, direct):
    pick = picker(counts, 1, grad_out.shape[0])[RELAYED:]
    for tile in tiles(grad_out.shape[1]):
        direct[:, tile] = dot(pick, grad_out[:, tile]).astype(BF16)


def pick_hidden(counts, hidden, far, near):
    rows, units = hidden.shape
    columns = half_of(lax.axis_index("loc"), units // 2)
    for index, out in ((2, far), (1, near)):
        out[...] = dot(hidden[:, columns], picker(counts, index, rows), (0, 1)).astype(BF16)


def pick_own(counts, hidden, own, places, mask):
    rows, units = hidden.shape
    pick = picker(counts, 0, rows)
    for tile in tiles(units):
        own[tile, :] = dot(hidden[:, tile], pick, (0, 1)).astype(BF16)
    for index in range(2):
        places[:, index * CAP : (index + 1) * CAP] = placer(counts, index, rows)
    place = lax.broadcasted_iota(jnp.int32, mask.shape, 0)
    mask[...] = (place >= CAP - counts[0, LAST]).astype(BF16)


def product_away(grad, weights, away):
    half = weights.shape[1] // 2
    away[...] = dot(grad[:CAP, :], weights[0, half_of(1 - lax.axis_index("loc"), half), :], (1, 1))


def product_here(grad, weights, here):
    half = weights.shape[1] // 2
    here[...] = dot(grad[:CAP, :], weights[0, half_of(lax.axis_index("loc"), half), :], (1, 1))


def join_near(turned, relayed, direct, weights, near, away):
    odd = lax.axis_index("grp") % 2 == 1

    @pl.when(odd)
    def _():
        near[:RELAYED, :] = turned[...]

    @pl.when(jnp.logical_not(odd))
    def _():
        near[:RELAYED, :] = relayed[...]

    near[RELAYED:, :] = direct[...]
    product_away(near, weights, away)


def add_halves(here, other, out):
    out[...] = (here[...] + other[...]).astype(BF16)


def place_first(places, own, near, out):
    out[...] = (dot(places[:, :CAP], own[...]) + dot(places[:, CAP:], near[...])).astype(BF16)


def place_last(first, mask, early, late, out):
    rows = first.shape[0]
    group, size = lax.axis_index("grp"), lax.axis_size("grp")
    step = pl.program_id(0)

    @pl.when(step < rows // CAP - 1)
    def _():
        out[...] = first[half_of(step, CAP), :]

    @pl.when(step == rows // CAP - 1)
    def _():
        far = jnp.where((group % 2 == 1) | (group == size - 2), late[...], early[...])
        high = first[rows - CAP :, :].astype(F32)
        out[...] = (high + far.astype(F32) * mask[...].astype(F32)).astype(BF16)


def own_weights(own_hidden, own, total):
    for tile in tiles(own.shape[1]):
        total[:, tile] = dot(own_hidden[...], own[:CAP, tile])


def half_weights(side, far_hidden, near_hidden, far, near, before, *refs):
    out, token = refs[-2:]
    step = pl.program_id(0)
    rows = half_of(step, BLOCK)
    whole = half_of(side() * (far_hidden.shape[0] // BLOCK) + step, BLOCK)
    for tile in tiles(far.shape[1]):
        total = before[whole, tile] + dot(far_hidden[rows, :], far[:, tile])
        out[0, :, tile] = (total + dot(near_hidden[rows, :], near[:, tile])).astype(BF16)
    token[...] = jnp.zeros_like(token)


def rows_of_half(side, *operands, units, features, before=()):
    steps = units // 2 // BLOCK
    return pl.pallas_call(
        functools.partial(half_weights, side),
        out_shape=[jax.ShapeDtypeStruct((1, units, features), BF16), jax.ShapeDtypeStruct((16, 128), BF16)],
        grid=(steps,),
        in_specs=[VMEM] * len(operands) + [ANY] * len(before),
        out_specs=[pl.BlockSpec((1, BLOCK, features), lambda step: (0, side() * steps + step, 0)), VMEM],
        input_output_aliases={len(operands): 0} if before else {},
        cost_estimate=pl.CostEstimate(flops=10**10, bytes_accessed=10**3, transcendentals=0),
        compiler_params=pltpu.CompilerParams(vmem_limit_bytes=16 << 20),
        name="half_weights",
    )(*operands, *before)


def local(grad_out, hidden, weights, counts):
    size = lax.axis_size("grp")
    rows, features = grad_out.shape
    units = hidden.shape[1]
    half = units // 2

    by1 = [(g, (g + 1) % size) for g in range(size)]
    by2 = [(g, (g + 2) % size) for g in range(size)]
    back1 = [(b, a) for a, b in by1]
    back2 = [(b, a) for a, b in by2]
    turn = [(g, g ^ 1) for g in range(size)]
    even_by2 = by2[::2]

    def send(value, pairs):
        return lax.ppermute(value, "grp", pairs)

    def swap_cores(value):
        return lax.ppermute(value, "loc", [(0, 1), (1, 0)])

    partial = ((CAP, half), F32)
    block = ((CAP, half), BF16)
    far = grad_out[rows - CAP :]
    far_in = send(far, by2)
    (turned,) = call(pick_turned, [((RELAYED, features), BF16)], counts, grad_out, scalars=1, after=(far,))
    turned_in = send(turned, turn)

    (own_away,) = call(product_away, [partial], grad_out, weights, after=(turned,))
    own_other = swap_cores(own_away)
    (own_here,) = call(product_here, [partial], grad_out, weights, after=(own_away,))
    far_hidden, near_hidden = call(
        pick_hidden, [((half, CAP), BF16), ((half, CAP), BF16)], counts, hidden, scalars=1, after=(own_here,)
    )
    (direct,) = call(
        pick_direct, [((CAP - RELAYED, features), BF16)], counts, grad_out, scalars=1, after=(far_hidden,)
    )
    direct_in = send(direct, by1)
    (own_block,) = call(add_halves, [block], own_here, own_other, after=(direct,))

    turned_in, own_block = lax.optimization_barrier((turned_in, own_block))
    relayed_in = send(turned_in, even_by2)

    (far_away,) = call(product_away, [partial], far_in, weights, after=(turned_in,))
    far_other = swap_cores(far_away)
    (far_here,) = call(product_here, [partial], far_in, weights, after=(far_away,))
    far_hidden, near_hidden, far_here = lax.optimization_barrier((far_hidden, near_hidden, far_here))
    near_hidden_in = send(near_hidden, by1)
    far_hidden_in = send(far_hidden, by2)

    (far_block,) = call(add_halves, [block], far_here, far_other)
    far_back_early = send(far_block, back2[:-2:2])
    own_hidden, places, mask = call(
        pick_own, [((units, CAP), BF16), ((rows, 2 * CAP), BF16), block], counts, hidden, scalars=1, after=(far_block,)
    )
    near_in, near_away = call(
        join_near, [((CAP, features), BF16), partial], turned_in, relayed_in, direct_in, weights, after=(places,)
    )
    near_other = swap_cores(near_away)
    (near_here,) = call(product_here, [partial], near_in, weights, after=(near_away,))
    (near_block,) = call(add_halves, [block], near_here, near_other)
    near_back = send(near_block, back1)
    (total,) = call(own_weights, [((units, features), F32)], own_hidden, grad_out, after=(near_block,))
    (late_block,) = call(add_halves, [block], far_here, far_other, after=(total,))
    far_back_late = send(late_block, back2[1::2] + back2[-2:-1])

    near_hidden_in, far_hidden_in, late_block = lax.optimization_barrier((near_hidden_in, far_hidden_in, late_block))
    here, _ = rows_of_half(
        lambda: lax.axis_index("loc"), far_hidden_in, near_hidden_in, far_in, near_in, total, units=units, features=features
    )
    grad_weights, done = rows_of_half(
        lambda: 1 - lax.axis_index("loc"), swap_cores(far_hidden_in), swap_cores(near_hidden_in), far_in, near_in, total,
        units=units, features=features, before=(here,),
    )
    (first,) = call(place_first, [((rows, half), BF16)], places, own_block, near_back, after=(done,))
    (grad_hidden,) = call(
        place_last, [((rows, half), BF16)], first, mask, far_back_early, far_back_late,
        grid=(rows // CAP,), out_specs=[pl.BlockSpec((CAP, half), lambda step: (step, 0))],
    )
    return grad_hidden, grad_weights


def solution(mesh):
    return jax.shard_map(
        local,
        mesh=mesh,
        in_specs=(
            P(("rep", "grp"), "loc"),
            P(("rep", "grp"), None),
            P("grp", None, "loc"),
            P(("rep", "grp"), None),
        ),
        out_specs=(P(("rep", "grp"), "loc"), P(("rep", "grp"), None, "loc")),
        check_vma=False,
    )
```

```python
import functools

import jax
import jax.numpy as jnp
from jax import lax
from jax.experimental import pallas as pl
from jax.experimental.pallas import tpu as pltpu
from jax.sharding import PartitionSpec as P

CAP = 256
RELAYED = 128
HEAD = 128
LAST = 2
TILE = 256
BLOCK = 256
BF16, F32 = jnp.bfloat16, jnp.float32
VMEM = pl.BlockSpec(memory_space=pltpu.VMEM)
SMEM = pl.BlockSpec(memory_space=pltpu.SMEM)
ANY = pl.BlockSpec(memory_space=pl.ANY)


def call(kernel, outs, *operands, after=(), scalars=0, grid=None, out_specs=None, cost=10**10):
    def body(*refs):
        kernel(*refs[: len(operands)], *refs[len(operands) + len(after) :])

    extra = {} if grid is None else {"grid": grid}
    return pl.pallas_call(
        body,
        out_shape=[jax.ShapeDtypeStruct(shape, dtype) for shape, dtype in outs],
        in_specs=[SMEM] * scalars + [VMEM] * (len(operands) - scalars) + [ANY] * len(after),
        out_specs=[VMEM] * len(outs) if out_specs is None else out_specs,
        cost_estimate=pl.CostEstimate(flops=cost, bytes_accessed=10**3, transcendentals=0),
        compiler_params=pltpu.CompilerParams(vmem_limit_bytes=16 << 20),
        name=kernel.__name__,
        **extra,
    )(*operands, *after)


def dot(left, right, contract=(1, 0)):
    return lax.dot_general(left, right, ((contract[:1], contract[1:]), ((), ())), preferred_element_type=F32)


def half_of(which, extent):
    return pl.ds(pl.multiple_of(which * extent, extent), extent)


def segment(counts, index):
    first = jnp.int32(0)
    for earlier in range(index):
        first = first + counts[0, earlier]
    return first, counts[0, index]


def picked(counts, index, place, row, rows):
    first, count = segment(counts, index)
    if index == LAST:
        return (row == rows - CAP + place) & (place >= CAP - count)
    return (row == first + place) & (place < count)


def picker(counts, index, rows):
    place = lax.broadcasted_iota(jnp.int32, (CAP, rows), 0)
    row = lax.broadcasted_iota(jnp.int32, (CAP, rows), 1)
    return picked(counts, index, place, row, rows).astype(BF16)


def placer(counts, index, rows):
    row = lax.broadcasted_iota(jnp.int32, (rows, CAP), 0)
    place = lax.broadcasted_iota(jnp.int32, (rows, CAP), 1)
    return picked(counts, index, place, row, rows).astype(BF16)


def tiles(extent):
    return [slice(at, min(at + TILE, extent)) for at in range(0, extent, TILE)]


def pick_turned(counts, grad_out, turned):
    pick = picker(counts, 1, grad_out.shape[0])[:RELAYED]
    for tile in tiles(grad_out.shape[1]):
        turned[:, tile] = dot(pick, grad_out[:, tile]).astype(BF16)


def pick_direct(counts, grad_out, direct):
    pick = picker(counts, 1, grad_out.shape[0])[RELAYED:]
    for tile in tiles(grad_out.shape[1]):
        direct[:, tile] = dot(pick, grad_out[:, tile]).astype(BF16)


def pick_hidden(counts, hidden, far, near):
    rows, units = hidden.shape
    columns = half_of(lax.axis_index("loc"), units // 2)
    for index, out in ((2, far), (1, near)):
        out[...] = dot(hidden[:, columns], picker(counts, index, rows), (0, 1)).astype(BF16)


def pick_own(counts, hidden, own, places, mask):
    rows, units = hidden.shape
    pick = picker(counts, 0, rows)
    for tile in tiles(units):
        own[tile, :] = dot(hidden[:, tile], pick, (0, 1)).astype(BF16)
    for index in range(2):
        places[:, index * CAP : (index + 1) * CAP] = placer(counts, index, rows)
    place = lax.broadcasted_iota(jnp.int32, mask.shape, 0)
    mask[...] = (place >= CAP - counts[0, LAST]).astype(BF16)


def product_away(grad, weights, away):
    half = weights.shape[1] // 2
    away[...] = dot(grad[:CAP, :], weights[0, half_of(1 - lax.axis_index("loc"), half), :], (1, 1))


def product_here(grad, weights, here):
    half = weights.shape[1] // 2
    here[...] = dot(grad[:CAP, :], weights[0, half_of(lax.axis_index("loc"), half), :], (1, 1))


def join_near(turned, relayed, direct, weights, near, away):
    odd = lax.axis_index("grp") % 2 == 1

    @pl.when(odd)
    def _():
        near[:RELAYED, :] = turned[...]

    @pl.when(jnp.logical_not(odd))
    def _():
        near[:RELAYED, :] = relayed[...]

    near[RELAYED:, :] = direct[...]
    product_away(near, weights, away)


def take_rest(grad_out, rest):
    rest[...] = grad_out[grad_out.shape[0] - rest.shape[0] :, :]


def join_far(head, rest, weights, far, away):
    far[: head.shape[0], :] = head[...]
    far[head.shape[0] :, :] = rest[...]
    product_away(far, weights, away)


def add_halves(here, other, out):
    out[...] = (here[...] + other[...]).astype(BF16)


def late_results():
    group, size = lax.axis_index("grp"), lax.axis_size("grp")
    return (group % 2 == 1) | (group == size - 2)


def place(first, far, mask, sums, out, copied):
    low = first.shape[0] - CAP
    sums[:low, :] = first[:low, :]
    sums[low:, :] = (first[low:, :].astype(F32) + far[...].astype(F32) * mask[...].astype(F32)).astype(BF16)
    copy = pltpu.make_async_copy(sums, out, copied)
    copy.start()
    copy.wait()


def place_early(places, own, near, mask, far, done, out, first, sums, copied):
    first[...] = (dot(places[:, :CAP], own[...]) + dot(places[:, CAP:], near[...])).astype(BF16)
    pl.when(jnp.logical_not(late_results()))(lambda: place(first, far, mask, sums, out, copied))


def place_late(first, mask, far, before, out, sums, copied):
    pl.when(late_results())(lambda: place(first, far, mask, sums, out, copied))


def own_weights(own_hidden, own, total):
    for tile in tiles(own.shape[1]):
        total[:, tile] = dot(own_hidden[...], own[:CAP, tile])


def half_weights(side, far_hidden, near_hidden, far, near, before, *refs):
    out, token = refs[-2:]
    step = pl.program_id(0)
    rows = half_of(step, BLOCK)
    whole = half_of(side() * (far_hidden.shape[0] // BLOCK) + step, BLOCK)
    for tile in tiles(far.shape[1]):
        total = before[whole, tile] + dot(far_hidden[rows, :], far[:, tile])
        out[0, :, tile] = (total + dot(near_hidden[rows, :], near[:, tile])).astype(BF16)
    token[...] = jnp.zeros_like(token)


def rows_of_half(side, *operands, units, features, before=()):
    steps = units // 2 // BLOCK
    return pl.pallas_call(
        functools.partial(half_weights, side),
        out_shape=[jax.ShapeDtypeStruct((1, units, features), BF16), jax.ShapeDtypeStruct((16, 128), BF16)],
        grid=(steps,),
        in_specs=[VMEM] * len(operands) + [ANY] * len(before),
        out_specs=[pl.BlockSpec((1, BLOCK, features), lambda step: (0, side() * steps + step, 0)), VMEM],
        input_output_aliases={len(operands): 0} if before else {},
        cost_estimate=pl.CostEstimate(flops=10**10, bytes_accessed=10**3, transcendentals=0),
        compiler_params=pltpu.CompilerParams(vmem_limit_bytes=16 << 20),
        name="half_weights",
    )(*operands, *before)


def local(grad_out, hidden, weights, counts):
    size = lax.axis_size("grp")
    rows, features = grad_out.shape
    units = hidden.shape[1]
    half = units // 2

    by1 = [(g, (g + 1) % size) for g in range(size)]
    by2 = [(g, (g + 2) % size) for g in range(size)]
    back1 = [(b, a) for a, b in by1]
    back2 = [(b, a) for a, b in by2]
    turn = [(g, g ^ 1) for g in range(size)]
    even_by2 = by2[::2]

    def send(value, pairs):
        return lax.ppermute(value, "grp", pairs)

    def swap_cores(value):
        return lax.ppermute(value, "loc", [(0, 1), (1, 0)])

    partial = ((CAP, half), F32)
    block = ((CAP, half), BF16)
    head = grad_out[rows - CAP : rows - CAP + HEAD]
    head_in = send(head, by2)
    (turned,) = call(pick_turned, [((RELAYED, features), BF16)], counts, grad_out, scalars=1, after=(head,))
    turned_in = send(turned, turn)
    (rest,) = call(take_rest, [((CAP - HEAD, features), BF16)], grad_out, after=(turned,))
    rest_in = send(rest, by2)

    (own_away,) = call(product_away, [partial], grad_out, weights, after=(rest,))
    own_other = swap_cores(own_away)
    (own_here,) = call(product_here, [partial], grad_out, weights, after=(own_away,))
    far_hidden, near_hidden = call(
        pick_hidden, [((half, CAP), BF16), ((half, CAP), BF16)], counts, hidden, scalars=1, after=(own_here,)
    )
    (direct,) = call(
        pick_direct, [((CAP - RELAYED, features), BF16)], counts, grad_out, scalars=1, after=(far_hidden,)
    )
    direct_in = send(direct, by1)
    (own_block,) = call(add_halves, [block], own_here, own_other, after=(direct,))

    turned_in, own_block = lax.optimization_barrier((turned_in, own_block))
    relayed_in = send(turned_in, even_by2)

    far_in, far_away = call(
        join_far, [((CAP, features), BF16), partial], head_in, rest_in, weights, after=(turned_in,)
    )
    far_other = swap_cores(far_away)
    (far_here,) = call(product_here, [partial], far_in, weights, after=(far_away,))
    far_hidden, near_hidden, far_here = lax.optimization_barrier((far_hidden, near_hidden, far_here))
    near_hidden_in = send(near_hidden, by1)
    far_hidden_in = send(far_hidden, by2)

    (far_block,) = call(add_halves, [block], far_here, far_other)
    far_back_early = send(far_block, back2[:-2:2])
    own_hidden, places, mask = call(
        pick_own, [((units, CAP), BF16), ((rows, 2 * CAP), BF16), block], counts, hidden, scalars=1, after=(far_block,)
    )
    near_in, near_away = call(
        join_near, [((CAP, features), BF16), partial], turned_in, relayed_in, direct_in, weights, after=(places,)
    )
    near_other = swap_cores(near_away)
    (near_here,) = call(product_here, [partial], near_in, weights, after=(near_away,))
    (near_block,) = call(add_halves, [block], near_here, near_other)
    near_back = send(near_block, back1)
    (total,) = call(own_weights, [((units, features), F32)], own_hidden, grad_out, after=(near_block,))
    (late_block,) = call(add_halves, [block], far_here, far_other, after=(total,))
    far_back_late = send(late_block, back2[1::2] + back2[-2:-1])

    near_hidden_in, far_hidden_in, late_block = lax.optimization_barrier((near_hidden_in, far_hidden_in, late_block))
    here, _ = rows_of_half(
        lambda: lax.axis_index("loc"), far_hidden_in, near_hidden_in, far_in, near_in, total, units=units, features=features
    )
    grad_weights, done = rows_of_half(
        lambda: 1 - lax.axis_index("loc"), swap_cores(far_hidden_in), swap_cores(near_hidden_in), far_in, near_in, total,
        units=units, features=features, before=(here,),
    )
    whole = jax.ShapeDtypeStruct((rows, half), BF16)
    common = {
        "scratch_shapes": [pltpu.VMEM((rows, half), BF16), pltpu.SemaphoreType.DMA],
        "cost_estimate": pl.CostEstimate(flops=10**10, bytes_accessed=10**3, transcendentals=0),
        "compiler_params": pltpu.CompilerParams(vmem_limit_bytes=16 << 20),
    }
    placed, first = pl.pallas_call(
        place_early, out_shape=[whole, whole], in_specs=[VMEM] * 5 + [ANY], out_specs=[ANY, VMEM], name="place_early", **common
    )(places, own_block, near_back, mask, far_back_early, done)
    grad_hidden = pl.pallas_call(
        place_late, out_shape=whole, in_specs=[VMEM] * 3 + [ANY], out_specs=ANY, input_output_aliases={3: 0},
        name="place_late", **common,
    )(first, mask, far_back_late, placed)
    return grad_hidden, grad_weights


def solution(mesh):
    return jax.shard_map(
        local,
        mesh=mesh,
        in_specs=(
            P(("rep", "grp"), "loc"),
            P(("rep", "grp"), None),
            P("grp", None, "loc"),
            P(("rep", "grp"), None),
        ),
        out_specs=(P(("rep", "grp"), "loc"), P(("rep", "grp"), None, "loc")),
        check_vma=False,
    )
```

```python
import functools

import jax
import jax.numpy as jnp
from jax import lax
from jax.experimental import pallas as pl
from jax.experimental.pallas import tpu as pltpu
from jax.sharding import PartitionSpec as P

CAP = 256
RELAYED = 128
HEAD = 128
LAST = 2
TILE = 256
BLOCK = 256
BF16, F32 = jnp.bfloat16, jnp.float32
VMEM = pl.BlockSpec(memory_space=pltpu.VMEM)
SMEM = pl.BlockSpec(memory_space=pltpu.SMEM)
ANY = pl.BlockSpec(memory_space=pl.ANY)


def call(kernel, outs, *operands, after=(), scalars=0, grid=None, out_specs=None, cost=10**10):
    def body(*refs):
        kernel(*refs[: len(operands)], *refs[len(operands) + len(after) :])

    extra = {} if grid is None else {"grid": grid}
    return pl.pallas_call(
        body,
        out_shape=[jax.ShapeDtypeStruct(shape, dtype) for shape, dtype in outs],
        in_specs=[SMEM] * scalars + [VMEM] * (len(operands) - scalars) + [ANY] * len(after),
        out_specs=[VMEM] * len(outs) if out_specs is None else out_specs,
        cost_estimate=pl.CostEstimate(flops=cost, bytes_accessed=10**3, transcendentals=0),
        compiler_params=pltpu.CompilerParams(vmem_limit_bytes=16 << 20),
        name=kernel.__name__,
        **extra,
    )(*operands, *after)


def dot(left, right, contract=(1, 0)):
    return lax.dot_general(left, right, ((contract[:1], contract[1:]), ((), ())), preferred_element_type=F32)


def half_of(which, extent):
    return pl.ds(pl.multiple_of(which * extent, extent), extent)


def segment(counts, index):
    first = jnp.int32(0)
    for earlier in range(index):
        first = first + counts[0, earlier]
    return first, counts[0, index]


def picked(counts, index, place, row, rows):
    first, count = segment(counts, index)
    if index == LAST:
        return (row == rows - CAP + place) & (place >= CAP - count)
    return (row == first + place) & (place < count)


def picker(counts, index, rows):
    place = lax.broadcasted_iota(jnp.int32, (CAP, rows), 0)
    row = lax.broadcasted_iota(jnp.int32, (CAP, rows), 1)
    return picked(counts, index, place, row, rows).astype(BF16)


def placer(counts, index, rows):
    row = lax.broadcasted_iota(jnp.int32, (rows, CAP), 0)
    place = lax.broadcasted_iota(jnp.int32, (rows, CAP), 1)
    return picked(counts, index, place, row, rows).astype(BF16)


def tiles(extent):
    return [slice(at, min(at + TILE, extent)) for at in range(0, extent, TILE)]


def pick_turned(counts, grad_out, turned):
    pick = picker(counts, 1, grad_out.shape[0])[:RELAYED]
    for tile in tiles(grad_out.shape[1]):
        turned[:, tile] = dot(pick, grad_out[:, tile]).astype(BF16)


def pick_direct(counts, grad_out, direct):
    pick = picker(counts, 1, grad_out.shape[0])[RELAYED:]
    for tile in tiles(grad_out.shape[1]):
        direct[:, tile] = dot(pick, grad_out[:, tile]).astype(BF16)


def pick_hidden(counts, hidden, far, near):
    rows, units = hidden.shape
    columns = half_of(lax.axis_index("loc"), units // 2)
    for index, out in ((2, far), (1, near)):
        out[...] = dot(hidden[:, columns], picker(counts, index, rows), (0, 1)).astype(BF16)


def pick_own(counts, hidden, own, places, mask):
    rows, units = hidden.shape
    pick = picker(counts, 0, rows)
    for tile in tiles(units):
        own[tile, :] = dot(hidden[:, tile], pick, (0, 1)).astype(BF16)
    for index in range(2):
        places[:, index * CAP : (index + 1) * CAP] = placer(counts, index, rows)
    place = lax.broadcasted_iota(jnp.int32, mask.shape, 0)
    mask[...] = (place >= CAP - counts[0, LAST]).astype(BF16)


def product_away(grad, weights, away):
    half = weights.shape[1] // 2
    away[...] = dot(grad[:CAP, :], weights[0, half_of(1 - lax.axis_index("loc"), half), :], (1, 1))


def product_here(grad, weights, here):
    half = weights.shape[1] // 2
    here[...] = dot(grad[:CAP, :], weights[0, half_of(lax.axis_index("loc"), half), :], (1, 1))


def product_part(part, grad, weights, away):
    quarter = away.shape[1]
    rows = half_of(2 * (1 - lax.axis_index("loc")) + part, quarter)
    away[...] = dot(grad[:CAP, :], weights[0, rows, :], (1, 1))


def product_rest(grad, weights, away):
    product_part(1, grad, weights, away)


def join_near(turned, relayed, direct, weights, near, away):
    odd = lax.axis_index("grp") % 2 == 1

    @pl.when(odd)
    def _():
        near[:RELAYED, :] = turned[...]

    @pl.when(jnp.logical_not(odd))
    def _():
        near[:RELAYED, :] = relayed[...]

    near[RELAYED:, :] = direct[...]
    product_part(0, near, weights, away)


def add_parts(here, left, right, out):
    quarter = left.shape[1]
    out[:, :quarter] = (here[:, :quarter] + left[...]).astype(BF16)
    out[:, quarter:] = (here[:, quarter:] + right[...]).astype(BF16)


def take_rest(grad_out, rest):
    rest[...] = grad_out[grad_out.shape[0] - rest.shape[0] :, :]


def join_far(head, rest, weights, far, away):
    far[: head.shape[0], :] = head[...]
    far[head.shape[0] :, :] = rest[...]
    product_away(far, weights, away)


def add_halves(here, other, out):
    out[...] = (here[...] + other[...]).astype(BF16)


def late_results():
    group, size = lax.axis_index("grp"), lax.axis_size("grp")
    return (group % 2 == 1) | (group == size - 2)


def place(first, far, mask, sums, out, copied):
    low = first.shape[0] - CAP
    head = pltpu.make_async_copy(first.at[pl.ds(0, low)], out.at[pl.ds(0, low)], copied.at[0])
    head.start()
    sums[...] = (first[low:, :].astype(F32) + far[...].astype(F32) * mask[...].astype(F32)).astype(BF16)
    last = pltpu.make_async_copy(sums, out.at[pl.ds(low, CAP)], copied.at[1])
    last.start()
    head.wait()
    last.wait()


def place_early(places, own, near, mask, far, done, out, first, sums, copied):
    first[...] = (dot(places[:, :CAP], own[...]) + dot(places[:, CAP:], near[...])).astype(BF16)
    pl.when(jnp.logical_not(late_results()))(lambda: place(first, far, mask, sums, out, copied))


def place_late(first, mask, far, before, out, sums, copied):
    pl.when(late_results())(lambda: place(first, far, mask, sums, out, copied))


def own_weights(own_hidden, own, total):
    for tile in tiles(own.shape[1]):
        total[:, tile] = dot(own_hidden[...], own[:CAP, tile])


def half_weights(side, far_hidden, near_hidden, far, near, before, *refs):
    out, token = refs[-2:]
    step = pl.program_id(0)
    rows = half_of(step, BLOCK)
    whole = half_of(side() * (far_hidden.shape[0] // BLOCK) + step, BLOCK)
    for tile in tiles(far.shape[1]):
        total = before[whole, tile] + dot(far_hidden[rows, :], far[:, tile])
        out[0, :, tile] = (total + dot(near_hidden[rows, :], near[:, tile])).astype(BF16)
    token[...] = jnp.zeros_like(token)


def rows_of_half(side, *operands, units, features, before=()):
    steps = units // 2 // BLOCK
    return pl.pallas_call(
        functools.partial(half_weights, side),
        out_shape=[jax.ShapeDtypeStruct((1, units, features), BF16), jax.ShapeDtypeStruct((16, 128), BF16)],
        grid=(steps,),
        in_specs=[VMEM] * len(operands) + [ANY] * len(before),
        out_specs=[pl.BlockSpec((1, BLOCK, features), lambda step: (0, side() * steps + step, 0)), VMEM],
        input_output_aliases={len(operands): 0} if before else {},
        cost_estimate=pl.CostEstimate(flops=10**10, bytes_accessed=10**3, transcendentals=0),
        compiler_params=pltpu.CompilerParams(vmem_limit_bytes=16 << 20),
        name="half_weights",
    )(*operands, *before)


def local(grad_out, hidden, weights, counts):
    size = lax.axis_size("grp")
    rows, features = grad_out.shape
    units = hidden.shape[1]
    half = units // 2

    by1 = [(g, (g + 1) % size) for g in range(size)]
    by2 = [(g, (g + 2) % size) for g in range(size)]
    back1 = [(b, a) for a, b in by1]
    back2 = [(b, a) for a, b in by2]
    turn = [(g, g ^ 1) for g in range(size)]
    even_by2 = by2[::2]

    def send(value, pairs):
        return lax.ppermute(value, "grp", pairs)

    def swap_cores(value):
        return lax.ppermute(value, "loc", [(0, 1), (1, 0)])

    partial = ((CAP, half), F32)
    block = ((CAP, half), BF16)
    head = grad_out[rows - CAP : rows - CAP + HEAD]
    head_in = send(head, by2)
    (turned,) = call(pick_turned, [((RELAYED, features), BF16)], counts, grad_out, scalars=1, after=(head,))
    turned_in = send(turned, turn)
    (rest,) = call(take_rest, [((CAP - HEAD, features), BF16)], grad_out, after=(turned,))
    rest_in = send(rest, by2)

    (own_away,) = call(product_away, [partial], grad_out, weights, after=(rest,))
    own_other = swap_cores(own_away)
    (own_here,) = call(product_here, [partial], grad_out, weights, after=(own_away,))
    far_hidden, near_hidden = call(
        pick_hidden, [((half, CAP), BF16), ((half, CAP), BF16)], counts, hidden, scalars=1, after=(own_here,)
    )
    (direct,) = call(
        pick_direct, [((CAP - RELAYED, features), BF16)], counts, grad_out, scalars=1, after=(far_hidden,)
    )
    direct_in = send(direct, by1)
    (own_block,) = call(add_halves, [block], own_here, own_other, after=(direct,))

    turned_in, own_block = lax.optimization_barrier((turned_in, own_block))
    relayed_in = send(turned_in, even_by2)

    far_in, far_away = call(
        join_far, [((CAP, features), BF16), partial], head_in, rest_in, weights, after=(turned_in,)
    )
    far_other = swap_cores(far_away)
    (far_here,) = call(product_here, [partial], far_in, weights, after=(far_away,))
    far_hidden, near_hidden, far_here = lax.optimization_barrier((far_hidden, near_hidden, far_here))
    near_hidden_in = send(near_hidden, by1)
    far_hidden_in = send(far_hidden, by2)

    (far_block,) = call(add_halves, [block], far_here, far_other)
    far_back_early = send(far_block, back2[:-2:2])
    own_hidden, places, mask = call(
        pick_own, [((units, CAP), BF16), ((rows, 2 * CAP), BF16), block], counts, hidden, scalars=1, after=(far_block,)
    )
    quarter = ((CAP, half // 2), F32)
    near_in, near_left = call(
        join_near, [((CAP, features), BF16), quarter], turned_in, relayed_in, direct_in, weights, after=(places,)
    )
    near_left_other = swap_cores(near_left)
    (near_right,) = call(product_rest, [quarter], near_in, weights, after=(near_left,))
    near_right_other = swap_cores(near_right)
    (near_here,) = call(product_here, [partial], near_in, weights, after=(near_right,))
    (near_block,) = call(add_parts, [block], near_here, near_left_other, near_right_other)
    near_back = send(near_block, back1)
    (total,) = call(own_weights, [((units, features), F32)], own_hidden, grad_out, after=(near_block,))
    (late_block,) = call(add_halves, [block], far_here, far_other, after=(total,))
    far_back_late = send(late_block, back2[1::2] + back2[-2:-1])

    near_hidden_in, far_hidden_in, late_block = lax.optimization_barrier((near_hidden_in, far_hidden_in, late_block))
    here, _ = rows_of_half(
        lambda: lax.axis_index("loc"), far_hidden_in, near_hidden_in, far_in, near_in, total, units=units, features=features
    )
    grad_weights, done = rows_of_half(
        lambda: 1 - lax.axis_index("loc"), swap_cores(far_hidden_in), swap_cores(near_hidden_in), far_in, near_in, total,
        units=units, features=features, before=(here,),
    )
    whole = jax.ShapeDtypeStruct((rows, half), BF16)
    common = {
        "scratch_shapes": [pltpu.VMEM((CAP, half), BF16), pltpu.SemaphoreType.DMA((2,))],
        "cost_estimate": pl.CostEstimate(flops=10**10, bytes_accessed=10**3, transcendentals=0),
        "compiler_params": pltpu.CompilerParams(vmem_limit_bytes=16 << 20),
    }
    placed, first = pl.pallas_call(
        place_early, out_shape=[whole, whole], in_specs=[VMEM] * 5 + [ANY], out_specs=[ANY, VMEM], name="place_early", **common
    )(places, own_block, near_back, mask, far_back_early, done)
    grad_hidden = pl.pallas_call(
        place_late, out_shape=whole, in_specs=[VMEM] * 3 + [ANY], out_specs=ANY, input_output_aliases={3: 0},
        name="place_late", **common,
    )(first, mask, far_back_late, placed)
    return grad_hidden, grad_weights


def solution(mesh):
    return jax.shard_map(
        local,
        mesh=mesh,
        in_specs=(
            P(("rep", "grp"), "loc"),
            P(("rep", "grp"), None),
            P("grp", None, "loc"),
            P(("rep", "grp"), None),
        ),
        out_specs=(P(("rep", "grp"), "loc"), P(("rep", "grp"), None, "loc")),
        check_vma=False,
    )
```
